32 devices in a mesh: layers: 2 (over y), gr: 4 (over z), gc: 4 (over x, core).
Axes of the slice: x: 2, y: 2, z: 4, core: 2. Of those that a mesh axis runs over, the one named last changes fastest.
Arguments:
- acts: bfloat16 [1536, 8192], P('layers', 'gc'), parts along dimension 0, may hold values from -6 to 6
- grads: bfloat16 [1536, 28672], P(('layers', 'gc'), 'gr'), parts along dimension 0, may hold values from -6 to 6
- act_basis: bfloat16 [16384, 8192], P(('layers', 'gc'), 'gr'), parts along dimension 0, may hold values from -0.0625 to 0.0625
- grad_basis: bfloat16 [57344, 14336], P(('layers', 'gr'), 'gc'), parts along dimension 0, may hold values from -0.03125 to 0.03125
Outputs:
- correction: bfloat16 [16384, 14336], P(('layers', 'gr'), 'gc'), parts along dimension 0
The draws below stay inside these ranges and needn't reach their ends.
There are 2 independent parts, one for each index of `layers`. The reference program is written for one: setup_inputs(seed, part) draws one part's arguments, and reference() takes and returns one part's arrays. A program takes and returns all parts, laid end to end along the dimension named above; each array names one. Nothing has to cross between parts.
All inputs are finite; a program needn't handle non-finite values.
Results may differ from the reference program's by a relative error of at most 0.0034.
Values may be sent and summed in bfloat16 or wider, within the bound.
No kernel may reach another device: no remote copies, remote signals or barrier semaphores. Data moves between devices by JAX's collectives and lax.ppermute only.
A program may use at most 192 MiB of HBM per device.

```python
import jax
import jax.numpy as jnp
from jax import lax

DIN = 8192
DOUT = 28672
KG = 14336
TOKENS = 768


def block_levels(own_key, dims, cuts, least, largest):
    loudness = 1.0
    for axis_at, parts in cuts:
        draws = jax.random.uniform(jax.random.fold_in(jax.random.fold_in(own_key, 6), axis_at), (parts,), jnp.float32, least / len(cuts), largest / len(cuts))
        loudness = loudness * jnp.repeat(jnp.exp(draws), dims[axis_at] // parts).reshape((-1,) + (1,) * (len(dims) - 1 - axis_at))
    return loudness


def gaussian(rng, shape, deviation, limit, shards=(), dtype=jnp.bfloat16):
    loudness = block_levels(rng, shape, shards, -0.22, 0.18) if shards else 1.0
    array = jax.random.normal(rng, shape, jnp.float32) * deviation * loudness
    return jnp.minimum(jnp.maximum(array, -limit), limit).astype(dtype)


def setup_inputs(seed: int = 0, part: int = 0) -> dict:
    key_list = jax.random.split(jax.random.key(seed), 5)
    part_keys = jax.random.split(jax.random.fold_in(key_list[4], part), 5)
    acts = gaussian(part_keys[0], (TOKENS, DIN), 1.0, 6.0, ((1, 4),))
    grads = gaussian(part_keys[1], (TOKENS, DOUT), 1.0, 6.0, ((0, 4), (1, 4)))
    act_basis = gaussian(part_keys[2], (DIN, DIN), DIN ** -0.5, 0.0625, ((0, 4), (1, 4)))
    grad_basis = gaussian(part_keys[3], (DOUT, KG), DOUT ** -0.5, 0.03125, ((0, 4), (1, 4)))
    return {"acts": acts, "grads": grads, "act_basis": act_basis, "grad_basis": grad_basis}


def reference(acts, grads, act_basis, grad_basis):
    proj_act = jnp.dot(acts, act_basis, preferred_element_type=jnp.float32)
    act_sq = (proj_act * proj_act).astype(jnp.bfloat16)
    proj_grad = jnp.dot(grads, grad_basis, preferred_element_type=jnp.float32)
    grad_sq = (proj_grad * proj_grad).astype(jnp.bfloat16)
    total = lax.dot_general(act_sq, grad_sq, (((0,), (0,)), ((), ())), preferred_element_type=jnp.float32)
    return (total / TOKENS).astype(jnp.bfloat16)
```

```python
import functools

import jax
import jax.numpy as jnp
from jax import lax
from jax.experimental import pallas as pl
from jax.experimental.pallas import tpu as pltpu
from jax.sharding import PartitionSpec as P

BF16 = jnp.bfloat16
F32 = jnp.float32
MIB = 2**20


def token_product(left, right):
    return lax.dot_general(
        left, right, (((0,), (0,)), ((), ())), preferred_element_type=F32
    )


def gathered(acts, grads, act_basis, grad_basis):
    token_count = acts.shape[0]
    grad_partial = jnp.dot(
        lax.all_gather(grads, "gc", axis=0, tiled=True),
        grad_basis,
        preferred_element_type=F32,
    )
    act_share = lax.psum_scatter(
        jnp.dot(acts, act_basis, preferred_element_type=F32),
        "gc",
        scatter_dimension=0,
        tiled=True,
    )
    act_sq = (act_share * act_share).astype(BF16)
    grad_share = lax.psum_scatter(grad_partial, "gr", scatter_dimension=0, tiled=True)
    grad_sq = (grad_share * grad_share).astype(BF16)
    grad_all = lax.all_gather(grad_sq, "gr", axis=0, tiled=True)
    total = token_product(lax.all_gather(act_sq, "gc", axis=0, tiled=True), grad_all)
    return (total / token_count).astype(BF16)


FREE = pl.CostEstimate(flops=10**7, bytes_accessed=10**5, transcendentals=0)
VMEM = pl.BlockSpec(memory_space=pltpu.VMEM)
ANYWHERE = pl.BlockSpec(memory_space=pl.ANY)


def ordered(array, *after):
    def body(*refs):
        pass

    return pl.pallas_call(
        body,
        in_specs=[ANYWHERE] * (1 + len(after)),
        out_specs=ANYWHERE,
        out_shape=jax.ShapeDtypeStruct(array.shape, array.dtype),
        input_output_aliases={0: 0},
        cost_estimate=FREE,
        name="ordered",
    )(array, *after)


def whole(body, out_shape, flags, arrays, after, name, limit=16):
    def run(flags_ref, *refs):
        body(flags_ref, *refs[:len(arrays)], *refs[len(arrays) + len(after):])

    return pl.pallas_call(
        run,
        in_specs=[pl.BlockSpec(memory_space=pltpu.SMEM)] + [VMEM] * len(arrays) + [ANYWHERE] * len(after),
        out_specs=[VMEM] * len(out_shape),
        out_shape=[pltpu.VMEM(shape, BF16) for shape in out_shape],
        compiler_params=pltpu.CompilerParams(vmem_limit_bytes=limit * MIB),
        name=name,
    )(flags, *arrays, *after)


def add_body(flags, left, right, out):
    out[...] = (left[...].astype(F32) + right[...].astype(F32)).astype(BF16)


def square_body(flags, left, right, out):
    t = left[...].astype(F32) + right[...].astype(F32)
    out[...] = (t * t).astype(BF16)


def square_or_term_body(flags, left, right, term, out):
    @pl.when(flags[0] == 0)
    def _():
        square_body(flags, left, right, out)

    @pl.when(flags[0] == 1)
    def _():
        out[...] = term[...]


def add_pieces_body(flags, keep, *refs):
    taken, out = refs[:-1], refs[-1]
    width = taken[0].shape[1]
    for i, piece in enumerate(taken):
        at = slice(i * width, (i + 1) * width)
        out[:, at] = (keep[:, at].astype(F32) + piece[...].astype(F32)).astype(BF16)


def square_pieces_body(flags, left, right, *outs):
    width = outs[0].shape[1]
    for i, out in enumerate(outs):
        at = slice(i * width, (i + 1) * width)
        t = left[:, at].astype(F32) + right[:, at].astype(F32)
        out[...] = (t * t).astype(BF16)


def stack_body(flags, *refs):
    n = len(refs) // 2
    own, other, out = refs[:n], refs[n:2 * n], refs[2 * n]
    block, width = own[0].shape[0] // 2, own[0].shape[1]
    for chip in range(2):
        @pl.when(flags[1] == chip)
        def _(chip=chip):
            for i in range(n):
                at = slice(i * width, (i + 1) * width)
                for to, which in ((0, chip), (2, 1 - chip)):
                    rows = slice(which * block, (which + 1) * block)
                    out[to * block:(to + 1) * block, at] = own[i][rows]
                    out[(to + 1) * block:(to + 2) * block, at] = other[i][rows]


def split(array, pieces, after):
    rows, columns = array.shape
    width = columns // pieces

    def body(array_ref, *refs):
        outs, sems = refs[len(after):-1], refs[-1]
        copies = [
            pltpu.make_async_copy(array_ref.at[:, pl.ds(i * width, width)], out, sems.at[i])
            for i, out in enumerate(outs)
        ]
        for copy in copies:
            copy.start()
        for copy in copies:
            copy.wait()

    return pl.pallas_call(
        body,
        in_specs=[ANYWHERE] * (1 + len(after)),
        out_specs=[VMEM] * pieces,
        out_shape=[pltpu.VMEM((rows, width), BF16)] * pieces,
        scratch_shapes=[pltpu.SemaphoreType.DMA((pieces,))],
        compiler_params=pltpu.CompilerParams(vmem_limit_bytes=16 * MIB),
        cost_estimate=FREE,
        name="split",
    )(array, *after)


def join(top, bottom, after):
    count, depth = top.shape
    width = depth // len(bottom)

    def body(top_ref, *refs):
        out, sems = refs[len(bottom) + len(after):]
        copies = [pltpu.make_async_copy(top_ref, out.at[pl.ds(0, count)], sems.at[0])]
        for i in range(len(bottom)):
            to = out.at[pl.ds(count, count), pl.ds(i * width, width)]
            copies.append(pltpu.make_async_copy(refs[i], to, sems.at[1 + i]))
        for copy in copies:
            copy.start()
        for copy in copies:
            copy.wait()

    return pl.pallas_call(
        body,
        in_specs=[ANYWHERE] * (1 + len(bottom) + len(after)),
        out_specs=VMEM,
        out_shape=pltpu.VMEM((2 * count, depth), BF16),
        scratch_shapes=[pltpu.SemaphoreType.DMA((1 + len(bottom),))],
        compiler_params=pltpu.CompilerParams(vmem_limit_bytes=16 * MIB),
        cost_estimate=FREE,
        name="join",
    )(top, *bottom, *after)


def project(rows, basis, first, widths, after):
    count, depth = rows.shape
    step = 256
    steps = sum(widths) // step

    def body(rows_ref, basis_ref, *refs):
        outs = refs[len(after):]
        j = pl.program_id(0)
        part = jnp.dot(rows_ref[...], basis_ref[...], preferred_element_type=F32).astype(BF16)
        at = 0
        for out, width in zip(outs, widths):
            for h in range(width // step):
                @pl.when(j == at)
                def _(out=out, h=h):
                    out[:, h * step:(h + 1) * step] = part
                at += 1

    return pl.pallas_call(
        body,
        grid=(steps,),
        in_specs=[VMEM, pl.BlockSpec((depth, step), lambda j: (0, first // step + j))] + [ANYWHERE] * len(after),
        out_specs=[pl.BlockSpec((count, w), lambda j: (0, 0)) for w in widths],
        out_shape=[pltpu.VMEM((count, w), BF16) for w in widths],
        compiler_params=pltpu.CompilerParams(vmem_limit_bytes=16 * MIB),
        cost_estimate=FREE,
        name="project_grads",
    )(rows, basis, *after)


def project_acts(flags, acts, basis, after):
    count, depth = acts.shape
    width = basis.shape[1]
    block = count // 4
    step = 512
    steps = width // step

    def body(flags_ref, acts_ref, basis_ref, *refs):
        keep, *gives = refs[len(after):]
        j = pl.program_id(0)
        part = jnp.dot(acts_ref[...], basis_ref[...], preferred_element_type=F32).astype(BF16)
        for own in range(2):
            @pl.when(flags_ref[2] == own)
            def _(own=own):
                for chip in range(2):
                    to = slice(chip * block, (chip + 1) * block)
                    mine, other = 2 * chip + own, 2 * chip + 1 - own
                    keep[to, :] = part[mine * block:(mine + 1) * block]
                    for i, give in enumerate(gives):
                        @pl.when(j == i)
                        def _(give=give, to=to, other=other):
                            give[to, :] = part[other * block:(other + 1) * block]

    out = pl.BlockSpec((count // 2, step), lambda j, c: (0, j))
    return pl.pallas_call(
        body,
        grid_spec=pltpu.PrefetchScalarGridSpec(
            num_scalar_prefetch=1,
            grid=(steps,),
            in_specs=[
                pl.BlockSpec((count, depth), lambda j, c: (0, 0)),
                pl.BlockSpec((depth, step), lambda j, c: (0, j)),
            ]
            + [ANYWHERE] * len(after),
            out_specs=[out] + [pl.BlockSpec((count // 2, step), lambda j, c: (0, 0))] * steps,
        ),
        out_shape=[pltpu.VMEM((count // 2, width), BF16)] + [pltpu.VMEM((count // 2, step), BF16)] * steps,
        compiler_params=pltpu.CompilerParams(vmem_limit_bytes=24 * MIB),
        cost_estimate=FREE,
        name="project_acts",
    )(flags, pltpu.with_memory_space_constraint(acts, pltpu.HBM), pltpu.with_memory_space_constraint(basis, pltpu.HBM), *after)


def correct(flags, act_sq, pieces, first, total_width, result, after):
    tokens, height = act_sq.shape
    half, step = pieces[0][0].shape
    flat = [a for piece in pieces for a in piece]
    extra = list(after) if result is None else [result, *after]

    def body(flags_ref, act_ref, *refs):
        ins = refs[:len(flat)]
        out, done, grad_sq = refs[len(flat) + len(extra):]
        j = pl.program_id(0)

        @pl.when(j == 0)
        def _():
            done[...] = jnp.zeros_like(done)

        for i in range(len(pieces)):
            for from_other in range(2):
                @pl.when((j == i) & (flags_ref[0] == from_other))
                def _(i=i, from_other=from_other):
                    grad_sq[:half] = ins[4 * i + from_other][...]
                    grad_sq[half:] = ins[4 * i + 2 + from_other][...]
        total = token_product(act_ref[...], grad_sq[...])
        out[...] = (total * (1.0 / tokens)).astype(BF16)

    return pl.pallas_call(
        body,
        grid_spec=pltpu.PrefetchScalarGridSpec(
            num_scalar_prefetch=1,
            grid=(len(pieces),),
            in_specs=[VMEM] * (1 + len(flat)) + [ANYWHERE] * len(extra),
            out_specs=[pl.BlockSpec((height, step), lambda j, o: (0, first // step + j)), VMEM],
            scratch_shapes=[pltpu.VMEM((tokens, step), BF16)],
        ),
        out_shape=[pltpu.HBM((height, total_width), BF16), pltpu.VMEM((16, 128), BF16)],
        input_output_aliases={} if result is None else {2 + len(flat): 0},
        compiler_params=pltpu.CompilerParams(vmem_limit_bytes=24 * MIB),
        cost_estimate=FREE,
        name="correct",
    )(flags, act_sq, *flat, *extra)


CORES = [(0, 1), (1, 0), (2, 3), (3, 2)]
CHIPS = [(0, 2), (2, 0), (1, 3), (3, 1)]
OUTER = [(0, 1), (1, 0), (2, 3), (3, 2)]
INNER = [(1, 2), (2, 1), (5, 6), (6, 5), (0, 4), (4, 0), (3, 7), (7, 3)]


def lined(acts, grads, act_basis, grad_basis):
    chunk = 512
    lag = 3
    width = grad_basis.shape[1]
    half = width // chunk
    count = 2 * half
    place = lax.axis_index("gr")
    chip, core = lax.axis_index("gc") // 2, lax.axis_index("gc") % 2
    is_outer = (place == 0) | (place == 3)
    flags = jnp.stack([is_outer.astype(jnp.int32), chip.astype(jnp.int32), core.astype(jnp.int32)])

    near = lax.ppermute(grads, "gc", CORES)
    far = lax.ppermute(grads, "gc", CHIPS)

    last = ()
    parts, payloads, received, sums, others = [], [], [], [], []

    def project_next(rows, n):
        nonlocal last
        first = len(parts) * chunk % width
        parts.extend(project(rows, grad_basis, first, [chunk] * n, last))
        last = (parts[-1],)

    def send(k):
        nonlocal last
        j = k - lag
        if k < lag:
            payload = parts[k]
        else:
            shape = sums[j].shape
            if k < count:
                (payload,) = whole(
                    square_or_term_body, [shape], flags, [sums[j], others[j], parts[k]], last, "square"
                )
            else:
                (payload,) = whole(square_body, [shape], flags, [sums[j], others[j]], last, "square")
            last = (payload,)
        payloads.append(payload)
        received.append(lax.ppermute(payload, "gr", OUTER))

    def add(k):
        nonlocal last
        sums.extend(whole(add_body, [parts[k].shape], flags, [parts[k], received[k]], last, "add"))
        last = (sums[-1],)
        others.append(lax.ppermute(sums[-1], ("layers", "gr"), INNER))

    result = None
    done = 0

    def correct_next(n):
        nonlocal last, result, done
        pieces = [
            (payloads[j + lag], received[j + lag], payloads[half + j + lag], received[half + j + lag])
            for j in range(done, done + n)
        ]
        result, token = correct(flags, act_sq, pieces, done * chunk, width, result, last)
        last = (token,)
        done += n

    def small(body, shapes, arrays, name):
        nonlocal last
        out = whole(body, shapes, flags, arrays, last, name, 24)
        last = (out[-1],)
        return out

    rows = join(pltpu.with_memory_space_constraint(grads, pltpu.HBM), [near], last)
    last = (rows,)
    project_next(rows, 1)
    send(0)
    project_next(rows, 2)
    send(1)
    send(2)
    add(0)
    project_next(rows, 2)
    add(1)
    send(3)
    project_next(rows, 1)
    add(2)
    send(4)
    project_next(rows, 1)
    add(3)
    send(5)
    add(4)
    far_pieces = split(far, far.shape[1] // 1024, last)
    last = (far_pieces[-1],)
    far_near = [lax.ppermute(piece, "gc", CORES) for piece in far_pieces]
    keep, *give = project_acts(flags, acts, act_basis, last)
    last = (keep,)
    taken = [lax.ppermute(piece, "gc", CORES) for piece in give]
    send(6)
    rows = join(far, far_near, last)
    last = (rows,)
    project_next(rows, 1)
    add(5)
    (act,) = small(add_pieces_body, [keep.shape], [keep, *taken], "add")
    act_far = lax.ppermute(act, "gc", CHIPS)
    send(7)
    project_next(rows, 2)
    add(6)
    send(8)
    add(7)
    project_next(rows, 2)
    send(9)
    add(8)
    project_next(rows, 1)
    send(10)
    add(9)
    project_next(rows, 1)
    send(11)
    add(10)
    own = small(square_pieces_body, [piece.shape for piece in give], [act, act_far], "square")
    other = [lax.ppermute(piece, "gc", CORES) for piece in own]
    send(12)
    add(11)
    (act_sq,) = small(stack_body, [(2 * act.shape[0], act.shape[1])], [*own, *other], "stack")
    send(13)
    correct_next(1)
    add(12)
    send(14)
    correct_next(2)
    add(13)
    send(15)
    correct_next(1)
    send(16)
    correct_next(1)
    correct_next(1)
    correct_next(1)
    return result


def solution(mesh):
    in_specs = (
        P("layers", "gc"),
        P(("layers", "gc"), "gr"),
        P(("layers", "gc"), "gr"),
        P(("layers", "gr"), "gc"),
    )
    out_specs = P(("layers", "gr"), "gc")
    sizes = (mesh.shape["layers"], mesh.shape["gr"], mesh.shape["gc"])
    shards = lined if sizes == (2, 4, 4) else gathered
    return jax.shard_map(shards, mesh=mesh, in_specs=in_specs, out_specs=out_specs, check_vma=False)
```

```python
import functools

import jax
import jax.numpy as jnp
from jax import lax
from jax.experimental import pallas as pl
from jax.experimental.pallas import tpu as pltpu
from jax.sharding import PartitionSpec as P

BF16 = jnp.bfloat16
F32 = jnp.float32
MIB = 2**20


def token_product(left, right):
    return lax.dot_general(
        left, right, (((0,), (0,)), ((), ())), preferred_element_type=F32
    )


def gathered(acts, grads, act_basis, grad_basis):
    token_count = acts.shape[0]
    grad_partial = jnp.dot(
        lax.all_gather(grads, "gc", axis=0, tiled=True),
        grad_basis,
        preferred_element_type=F32,
    )
    act_share = lax.psum_scatter(
        jnp.dot(acts, act_basis, preferred_element_type=F32),
        "gc",
        scatter_dimension=0,
        tiled=True,
    )
    act_sq = (act_share * act_share).astype(BF16)
    grad_share = lax.psum_scatter(grad_partial, "gr", scatter_dimension=0, tiled=True)
    grad_sq = (grad_share * grad_share).astype(BF16)
    grad_all = lax.all_gather(grad_sq, "gr", axis=0, tiled=True)
    total = token_product(lax.all_gather(act_sq, "gc", axis=0, tiled=True), grad_all)
    return (total / token_count).astype(BF16)


FREE = pl.CostEstimate(flops=10**7, bytes_accessed=10**5, transcendentals=0)
VMEM = pl.BlockSpec(memory_space=pltpu.VMEM)
ANYWHERE = pl.BlockSpec(memory_space=pl.ANY)


def ordered(array, *after):
    def body(*refs):
        pass

    return pl.pallas_call(
        body,
        in_specs=[ANYWHERE] * (1 + len(after)),
        out_specs=ANYWHERE,
        out_shape=jax.ShapeDtypeStruct(array.shape, array.dtype),
        input_output_aliases={0: 0},
        compiler_params=pltpu.CompilerParams(vmem_limit_bytes=MIB),
        cost_estimate=FREE,
        name="ordered",
    )(array, *after)


def whole(body, out_shape, flags, arrays, after, name, limit=8):
    def run(flags_ref, *refs):
        body(flags_ref, *refs[:len(arrays)], *refs[len(arrays) + len(after):])

    return pl.pallas_call(
        run,
        in_specs=[pl.BlockSpec(memory_space=pltpu.SMEM)] + [VMEM] * len(arrays) + [ANYWHERE] * len(after),
        out_specs=[VMEM] * len(out_shape),
        out_shape=[pltpu.VMEM(shape, BF16) for shape in out_shape],
        compiler_params=pltpu.CompilerParams(vmem_limit_bytes=limit * MIB),
        name=name,
    )(flags, *arrays, *after)


def add_body(flags, left, right, out):
    out[...] = (left[...].astype(F32) + right[...].astype(F32)).astype(BF16)


def square_body(flags, left, right, out):
    t = left[...].astype(F32) + right[...].astype(F32)
    out[...] = (t * t).astype(BF16)


def square_or_term_body(flags, left, right, term, out):
    @pl.when(flags[0] == 0)
    def _():
        square_body(flags, left, right, out)

    @pl.when(flags[0] == 1)
    def _():
        out[...] = term[...]


def add_pieces_body(flags, *refs):
    n = len(refs) // 2
    width = refs[0].shape[1]
    for i in range(n):
        add_body(flags, refs[i], refs[n + i], refs[2 * n].at[:, i * width:(i + 1) * width])


def square_pieces_body(flags, left, right, *outs):
    width = outs[0].shape[1]
    for i, out in enumerate(outs):
        at = slice(i * width, (i + 1) * width)
        square_body(flags, left.at[:, at], right.at[:, at], out)


def stack_body(flags, *refs):
    n = len(refs) // 2
    own, other, out = refs[:n], refs[n:2 * n], refs[2 * n]
    block, width = own[0].shape[0] // 2, own[0].shape[1]
    for chip in range(2):
        @pl.when(flags[1] == chip)
        def _(chip=chip):
            for i in range(n):
                rows = []
                for which in (chip, 1 - chip):
                    at = slice(which * block, (which + 1) * block)
                    rows += [own[i][at], other[i][at]]
                out[i * width:(i + 1) * width, :] = jnp.concatenate(rows).T


def split(array, widths, after):
    rows = array.shape[0]

    def body(array_ref, *refs):
        outs, sems = refs[len(after):-1], refs[-1]
        at, copies = 0, []
        for i, out in enumerate(outs):
            copies.append(pltpu.make_async_copy(array_ref.at[:, pl.ds(at, widths[i])], out, sems.at[i]))
            at += widths[i]
        start(copies)
        wait(copies)

    return pl.pallas_call(
        body,
        in_specs=[ANYWHERE] * (1 + len(after)),
        out_specs=[VMEM] * len(widths),
        out_shape=[pltpu.VMEM((rows, width), BF16) for width in widths],
        scratch_shapes=[pltpu.SemaphoreType.DMA((len(widths),))],
        compiler_params=pltpu.CompilerParams(vmem_limit_bytes=2 * MIB),
        cost_estimate=FREE,
        name="split",
    )(array, *after)


def join(top, bottom, after):
    count = top[0].shape[0]
    depth = sum(piece.shape[1] for piece in top)
    n = len(top) + len(bottom)

    def body(*refs):
        out, sems = refs[n + len(after):]
        copies = []
        for first, row, pieces in ((0, 0, top), (len(top), count, bottom)):
            at = 0
            for i, piece in enumerate(pieces):
                width = piece.shape[1]
                to = out.at[pl.ds(row, count), pl.ds(at, width)]
                copies.append(pltpu.make_async_copy(refs[first + i], to, sems.at[first + i]))
                at += width
        start(copies)
        wait(copies)

    return pl.pallas_call(
        body,
        in_specs=[ANYWHERE] * (n + len(after)),
        out_specs=VMEM,
        out_shape=pltpu.VMEM((2 * count, depth), BF16),
        scratch_shapes=[pltpu.SemaphoreType.DMA((n,))],
        compiler_params=pltpu.CompilerParams(vmem_limit_bytes=2 * MIB),
        cost_estimate=FREE,
        name="join",
    )(*top, *bottom, *after)


def block_copies(basis_ref, first, out, sems):
    parts = sems.shape[0]
    rows = out.shape[0] // parts
    return [
        pltpu.make_async_copy(
            basis_ref.at[pl.ds(i * rows, rows), pl.ds(first, out.shape[1])], out.at[pl.ds(i * rows, rows)], sems.at[i]
        )
        for i in range(parts)
    ]


def start(copies):
    for copy in copies:
        copy.start()


def wait(copies):
    for copy in copies:
        copy.wait()


COPIES = 7


def fetch(basis, width, after):
    depth = basis.shape[0]

    def body(basis_ref, *refs):
        out, sems = refs[len(after):]
        copies = block_copies(basis_ref, 0, out, sems)
        start(copies)
        wait(copies)

    return pl.pallas_call(
        body,
        in_specs=[ANYWHERE] * (1 + len(after)),
        out_specs=VMEM,
        out_shape=pltpu.VMEM((depth, width), BF16),
        scratch_shapes=[pltpu.SemaphoreType.DMA((COPIES,))],
        compiler_params=pltpu.CompilerParams(vmem_limit_bytes=2 * MIB),
        cost_estimate=FREE,
        name="fetch",
    )(basis, *after)


def project(rows, basis, block, then, after):
    count, depth = rows.shape
    width = block.shape[1]
    fetches = then is not None
    step = depth // 2

    def body(rows_ref, basis_ref, block_ref, *refs):
        refs = refs[len(after):]
        if fetches:
            ahead = block_copies(basis_ref, then, refs[1], refs[2])
            start(ahead)

        def add(i, total):
            at = pl.ds(pl.multiple_of(i * step, step), step)
            return total + jnp.dot(rows_ref[:, at], block_ref[at, :], preferred_element_type=F32)

        refs[0][...] = lax.fori_loop(0, depth // step, add, jnp.zeros((count, width), F32)).astype(BF16)
        if fetches:
            wait(ahead)

    shapes = [pltpu.VMEM((count, width), BF16)] + [pltpu.VMEM((depth, width), BF16)] * fetches
    return pl.pallas_call(
        body,
        in_specs=[VMEM, ANYWHERE, VMEM] + [ANYWHERE] * len(after),
        out_specs=[VMEM] * len(shapes),
        out_shape=shapes,
        scratch_shapes=[pltpu.SemaphoreType.DMA((COPIES,))] * fetches,
        compiler_params=pltpu.CompilerParams(vmem_limit_bytes=8 * MIB),
        cost_estimate=FREE,
        name="project_grads",
    )(rows, basis, block, *after)


def project_acts(flags, acts, basis, first, width, given, after):
    count, depth = acts.shape
    tokens = count // 4
    step = 512
    steps = width // step

    def body(flags_ref, acts_ref, basis_ref, *refs):
        given_refs, outs = refs[:len(given)], refs[len(given) + len(after):]
        keeps, gives = outs[:steps], outs[steps:]
        j = pl.program_id(0)

        @pl.when(j == 0)
        def _():
            for old, new in zip(given_refs, gives):
                new[...] = old[...]

        part = jnp.dot(acts_ref[...], basis_ref[...], preferred_element_type=F32).astype(BF16)
        for own in range(2):
            for i in range(steps):
                @pl.when((flags_ref[2] == own) & (j == i))
                def _(own=own, i=i):
                    for chip in range(2):
                        to = slice(chip * tokens, (chip + 1) * tokens)
                        mine, other = 2 * chip + own, 2 * chip + 1 - own
                        keeps[i][to, :] = part[mine * tokens:(mine + 1) * tokens]
                        gives[len(given) + i][to, :] = part[other * tokens:(other + 1) * tokens]

    n = 2 * steps + len(given)
    return pl.pallas_call(
        body,
        grid_spec=pltpu.PrefetchScalarGridSpec(
            num_scalar_prefetch=1,
            grid=(steps,),
            in_specs=[
                VMEM,
                pl.BlockSpec((depth, step), lambda j, c: (0, first // step + j)),
            ]
            + [VMEM] * len(given)
            + [ANYWHERE] * len(after),
            out_specs=[VMEM] * n,
        ),
        out_shape=[pltpu.VMEM((count // 2, step), BF16)] * n,
        compiler_params=pltpu.CompilerParams(vmem_limit_bytes=12 * MIB),
        cost_estimate=FREE,
        name="project_acts",
    )(
        flags,
        acts,
        pltpu.with_memory_space_constraint(basis, pltpu.HBM),
        *given,
        *after,
    )


def correct(flags, act_sq, pieces, first, total_width, result, after):
    height, tokens = act_sq.shape
    half, chunk = pieces[0][0].shape
    flat = [a for piece in pieces for a in piece]
    width = chunk * len(pieces)
    extra = list(after) if result is None else [result, *after]
    rows = height // (4 * len(pieces))

    def body(flags_ref, act_ref, *refs):
        ins = refs[:len(flat)]
        out, done, grad_sq, held, sems = refs[len(flat) + len(extra):]
        done[...] = jnp.zeros_like(done)
        for from_other in range(2):
            @pl.when(flags_ref[0] == from_other)
            def _(from_other=from_other):
                for i in range(len(pieces)):
                    at = slice(i * chunk, (i + 1) * chunk)
                    grad_sq[:half, at] = ins[4 * i + from_other][...]
                    grad_sq[half:, at] = ins[4 * i + 2 + from_other][...]

        def copy(r):
            at = pl.ds(pl.multiple_of(r * rows, rows), rows)
            slot = lax.rem(r, 2)
            return pltpu.make_async_copy(held.at[slot], out.at[at, pl.ds(first, width)], sems.at[slot])

        @pl.loop(0, height // rows)
        def _(r):
            act = act_ref[pl.ds(pl.multiple_of(r * rows, rows), rows), :]
            total = jnp.dot(act, grad_sq[...], preferred_element_type=F32)

            @pl.when(r >= 2)
            def _():
                copy(r - 2).wait()

            held[lax.rem(r, 2)] = (total * (1.0 / tokens)).astype(BF16)
            copy(r).start()

        copy(height // rows - 2).wait()
        copy(height // rows - 1).wait()

    return pl.pallas_call(
        body,
        in_specs=[pl.BlockSpec(memory_space=pltpu.SMEM)] + [VMEM] * (1 + len(flat)) + [ANYWHERE] * len(extra),
        out_specs=[ANYWHERE, VMEM],
        out_shape=[pltpu.HBM((height, total_width), BF16), pltpu.VMEM((16, 128), BF16)],
        scratch_shapes=[
            pltpu.VMEM((tokens, width), BF16),
            pltpu.VMEM((2, rows, width), BF16),
            pltpu.SemaphoreType.DMA((2,)),
        ],
        input_output_aliases={} if result is None else {2 + len(flat): 0},
        compiler_params=pltpu.CompilerParams(vmem_limit_bytes=12 * MIB),
        cost_estimate=FREE,
        name="correct",
    )(flags, act_sq, *flat, *extra)


CORES = [(0, 1), (1, 0), (2, 3), (3, 2)]
CHIPS = [(0, 2), (2, 0), (1, 3), (3, 1)]
OUTER = [(0, 1), (1, 0), (2, 3), (3, 2)]
INNER = [(1, 2), (2, 1), (5, 6), (6, 5), (0, 4), (4, 0), (3, 7), (7, 3)]


def lined(acts, grads, act_basis, grad_basis):
    chunk = 512
    lag = 3
    width = grad_basis.shape[1]
    half = width // chunk
    count = 2 * half
    place = lax.axis_index("gr")
    chip, core = lax.axis_index("gc") // 2, lax.axis_index("gc") % 2
    is_outer = (place == 0) | (place == 3)
    flags = jnp.stack([is_outer.astype(jnp.int32), chip.astype(jnp.int32), core.astype(jnp.int32)])

    near = lax.ppermute(grads, "gc", CORES)
    last = (flags,)
    block = None
    parts, payloads, received, sums, others = [], [], [], [], []

    def project_next(rows):
        nonlocal last, block
        k = len(parts)
        then = (k + 1) % half * chunk if k + 1 < count else None
        part, *blocks = project(rows, grad_basis, block, then, last)
        block = blocks[0] if blocks else None
        parts.append(part)
        last = (part,)

    def send(k):
        nonlocal last
        j = k - lag
        if k < lag:
            payload = parts[k]
        else:
            shape = sums[j].shape
            if k < count:
                (payload,) = whole(
                    square_or_term_body, [shape], flags, [sums[j], others[j], parts[k]], last, "square"
                )
            else:
                (payload,) = whole(square_body, [shape], flags, [sums[j], others[j]], last, "square")
            last = (payload,)
        payloads.append(payload)
        received.append(lax.ppermute(payload, "gr", OUTER))

    def add(k):
        nonlocal last
        sums.extend(whole(add_body, [parts[k].shape], flags, [parts[k], received[k]], last, "add"))
        last = (sums[-1],)
        others.append(lax.ppermute(sums[-1], ("layers", "gr"), INNER))

    result = None
    done = 0

    def correct_next(n):
        nonlocal last, result, done
        pieces = [
            (payloads[j + lag], received[j + lag], payloads[half + j + lag], received[half + j + lag])
            for j in range(done, done + n)
        ]
        result, token = correct(flags, act_sq, pieces, done * chunk, width, result, last)
        last = (token,)
        done += n

    def small(body, shapes, arrays, name):
        nonlocal last
        out = whole(body, shapes, flags, arrays, last, name)
        last = (out[-1],)
        return out

    far = lax.ppermute(grads, "gc", CHIPS)
    columns = act_basis.shape[1]
    block = fetch(grad_basis, chunk, last)
    last = (block,)
    act_terms = list(project_acts(flags, acts, act_basis, 0, columns, [], last))
    keep, give = act_terms[:len(act_terms) // 2], act_terms[len(act_terms) // 2:]
    last = (keep[-1],)
    taken = [lax.ppermute(piece, "gc", CORES) for piece in give]
    rows = join([pltpu.with_memory_space_constraint(grads, pltpu.HBM)], [near], last)
    last = (rows,)
    project_next(rows)
    send(0)
    project_next(rows)
    send(1)
    (act,) = small(add_pieces_body, [(keep[0].shape[0], columns)], [*keep, *taken], "add")
    act_far = lax.ppermute(act, "gc", CHIPS)
    project_next(rows)
    send(2)
    add(0)
    project_next(rows)
    for k in (1, 2, 3):
        add(k)
        project_next(rows)
        send(k + 2)
    far_pieces = split(far, [far.shape[1] // 7] * 7, last)
    last = (far_pieces[-1],)
    far_near = [lax.ppermute(piece, "gc", CORES) for piece in far_pieces]
    add(4)
    send(6)
    rows = join([far], far_near, last)
    last = (rows,)
    project_next(rows)
    add(5)
    send(7)
    for k in range(6, 12):
        add(k)
        project_next(rows)
        send(k + 2)
        if k == 9:
            own = small(square_pieces_body, [(act.shape[0], columns // 2)] * 2, [act, act_far], "square")
            other = [lax.ppermute(piece, "gc", CORES) for piece in own]
    add(12)
    send(14)
    (act_sq,) = small(stack_body, [(columns, 2 * act.shape[0])], [*own, *other], "stack")
    correct_next(1)
    add(13)
    send(15)
    correct_next(2)
    send(16)
    correct_next(2)
    correct_next(1)
    correct_next(1)
    return result


def solution(mesh):
    in_specs = (
        P("layers", "gc"),
        P(("layers", "gc"), "gr"),
        P(("layers", "gc"), "gr"),
        P(("layers", "gr"), "gc"),
    )
    out_specs = P(("layers", "gr"), "gc")
    sizes = (mesh.shape["layers"], mesh.shape["gr"], mesh.shape["gc"])
    shards = lined if sizes == (2, 4, 4) else gathered
    return jax.shard_map(shards, mesh=mesh, in_specs=in_specs, out_specs=out_specs, check_vma=False)
```

```python
import functools

import jax
import jax.numpy as jnp
from jax import lax
from jax.experimental import pallas as pl
from jax.experimental.pallas import tpu as pltpu
from jax.sharding import PartitionSpec as P

BF16 = jnp.bfloat16
F32 = jnp.float32
MIB = 2**20


def token_product(left, right):
    return lax.dot_general(
        left, right, (((0,), (0,)), ((), ())), preferred_element_type=F32
    )


def gathered(acts, grads, act_basis, grad_basis):
    token_count = acts.shape[0]
    grad_partial = jnp.dot(
        lax.all_gather(grads, "gc", axis=0, tiled=True),
        grad_basis,
        preferred_element_type=F32,
    )
    act_share = lax.psum_scatter(
        jnp.dot(acts, act_basis, preferred_element_type=F32),
        "gc",
        scatter_dimension=0,
        tiled=True,
    )
    act_sq = (act_share * act_share).astype(BF16)
    grad_share = lax.psum_scatter(grad_partial, "gr", scatter_dimension=0, tiled=True)
    grad_sq = (grad_share * grad_share).astype(BF16)
    grad_all = lax.all_gather(grad_sq, "gr", axis=0, tiled=True)
    total = token_product(lax.all_gather(act_sq, "gc", axis=0, tiled=True), grad_all)
    return (total / token_count).astype(BF16)


FREE = pl.CostEstimate(flops=10**7, bytes_accessed=10**5, transcendentals=0)
VMEM = pl.BlockSpec(memory_space=pltpu.VMEM)
ANYWHERE = pl.BlockSpec(memory_space=pl.ANY)


def ordered(array, *after):
    def body(*refs):
        pass

    return pl.pallas_call(
        body,
        in_specs=[ANYWHERE] * (1 + len(after)),
        out_specs=ANYWHERE,
        out_shape=jax.ShapeDtypeStruct(array.shape, array.dtype),
        input_output_aliases={0: 0},
        compiler_params=pltpu.CompilerParams(vmem_limit_bytes=MIB),
        cost_estimate=FREE,
        name="ordered",
    )(array, *after)


def whole(body, out_shape, flags, arrays, after, name, limit=8):
    def run(flags_ref, *refs):
        body(flags_ref, *refs[:len(arrays)], *refs[len(arrays) + len(after):])

    return pl.pallas_call(
        run,
        in_specs=[pl.BlockSpec(memory_space=pltpu.SMEM)] + [VMEM] * len(arrays) + [ANYWHERE] * len(after),
        out_specs=[VMEM] * len(out_shape),
        out_shape=[pltpu.VMEM(shape, BF16) for shape in out_shape],
        compiler_params=pltpu.CompilerParams(vmem_limit_bytes=limit * MIB),
        name=name,
    )(flags, *arrays, *after)


def add_body(flags, left, right, out):
    out[...] = (left[...].astype(F32) + right[...].astype(F32)).astype(BF16)


def square_body(flags, left, right, out):
    t = left[...].astype(F32) + right[...].astype(F32)
    out[...] = (t * t).astype(BF16)


def square_or_term_body(flags, left, right, term, out):
    @pl.when(flags[0] == 0)
    def _():
        square_body(flags, left, right, out)

    @pl.when(flags[0] == 1)
    def _():
        out[...] = term[...]


def add_pieces_body(flags, *refs):
    n = len(refs) // 2
    width = refs[0].shape[1]
    for i in range(n):
        add_body(flags, refs[i], refs[n + i], refs[2 * n].at[:, i * width:(i + 1) * width])


def square_pieces_body(flags, left, right, *outs):
    width = outs[0].shape[1]
    for i, out in enumerate(outs):
        at = slice(i * width, (i + 1) * width)
        square_body(flags, left.at[:, at], right.at[:, at], out)


def stack_body(flags, *refs):
    n = len(refs) // 2
    own, other, out = refs[:n], refs[n:2 * n], refs[2 * n]
    block, width = own[0].shape[0] // 2, own[0].shape[1]
    for chip in range(2):
        @pl.when(flags[1] == chip)
        def _(chip=chip):
            for i in range(n):
                rows = []
                for which in (chip, 1 - chip):
                    at = slice(which * block, (which + 1) * block)
                    rows += [own[i][at], other[i][at]]
                out[i * width:(i + 1) * width, :] = jnp.concatenate(rows).T


def split(array, widths, after):
    rows = array.shape[0]

    def body(array_ref, *refs):
        outs, sems = refs[len(after):-1], refs[-1]
        at, copies = 0, []
        for i, out in enumerate(outs):
            copies.append(pltpu.make_async_copy(array_ref.at[:, pl.ds(at, widths[i])], out, sems.at[i]))
            at += widths[i]
        start(copies)
        wait(copies)

    return pl.pallas_call(
        body,
        in_specs=[ANYWHERE] * (1 + len(after)),
        out_specs=[VMEM] * len(widths),
        out_shape=[pltpu.VMEM((rows, width), BF16) for width in widths],
        scratch_shapes=[pltpu.SemaphoreType.DMA((len(widths),))],
        compiler_params=pltpu.CompilerParams(vmem_limit_bytes=2 * MIB),
        cost_estimate=FREE,
        name="split",
    )(array, *after)


def join(top, bottom, after):
    count = top[0].shape[0]
    depth = sum(piece.shape[1] for piece in top)
    n = len(top) + len(bottom)

    def body(*refs):
        out, sems = refs[n + len(after):]
        copies = []
        for first, row, pieces in ((0, 0, top), (len(top), count, bottom)):
            at = 0
            for i, piece in enumerate(pieces):
                width = piece.shape[1]
                to = out.at[pl.ds(row, count), pl.ds(at, width)]
                copies.append(pltpu.make_async_copy(refs[first + i], to, sems.at[first + i]))
                at += width
        start(copies)
        wait(copies)

    return pl.pallas_call(
        body,
        in_specs=[ANYWHERE] * (n + len(after)),
        out_specs=VMEM,
        out_shape=pltpu.VMEM((2 * count, depth), BF16),
        scratch_shapes=[pltpu.SemaphoreType.DMA((n,))],
        compiler_params=pltpu.CompilerParams(vmem_limit_bytes=2 * MIB),
        cost_estimate=FREE,
        name="join",
    )(*top, *bottom, *after)


def block_copies(basis_ref, first, out, sems):
    parts = sems.shape[0]
    rows = out.shape[0] // parts
    return [
        pltpu.make_async_copy(
            basis_ref.at[pl.ds(i * rows, rows), pl.ds(first, out.shape[1])], out.at[pl.ds(i * rows, rows)], sems.at[i]
        )
        for i in range(parts)
    ]


def start(copies):
    for copy in copies:
        copy.start()


def wait(copies):
    for copy in copies:
        copy.wait()


COPIES = 7


def fetch(basis, width, after):
    depth = basis.shape[0]

    def body(basis_ref, *refs):
        out, sems = refs[len(after):]
        copies = block_copies(basis_ref, 0, out, sems)
        start(copies)
        wait(copies)

    return pl.pallas_call(
        body,
        in_specs=[ANYWHERE] * (1 + len(after)),
        out_specs=VMEM,
        out_shape=pltpu.VMEM((depth, width), BF16),
        scratch_shapes=[pltpu.SemaphoreType.DMA((COPIES,))],
        compiler_params=pltpu.CompilerParams(vmem_limit_bytes=2 * MIB),
        cost_estimate=FREE,
        name="fetch",
    )(basis, *after)


def project(rows, basis, block, then, after):
    count, depth = rows.shape
    width = block.shape[1]
    fetches = then is not None
    step = depth // 2

    def body(rows_ref, basis_ref, block_ref, *refs):
        refs = refs[len(after):]
        if fetches:
            ahead = block_copies(basis_ref, then, refs[1], refs[2])
            start(ahead)

        def add(i, total):
            at = pl.ds(pl.multiple_of(i * step, step), step)
            return total + jnp.dot(rows_ref[:, at], block_ref[at, :], preferred_element_type=F32)

        refs[0][...] = lax.fori_loop(0, depth // step, add, jnp.zeros((count, width), F32)).astype(BF16)
        if fetches:
            wait(ahead)

    shapes = [pltpu.VMEM((count, width), BF16)] + [pltpu.VMEM((depth, width), BF16)] * fetches
    return pl.pallas_call(
        body,
        in_specs=[VMEM, ANYWHERE, VMEM] + [ANYWHERE] * len(after),
        out_specs=[VMEM] * len(shapes),
        out_shape=shapes,
        scratch_shapes=[pltpu.SemaphoreType.DMA((COPIES,))] * fetches,
        compiler_params=pltpu.CompilerParams(vmem_limit_bytes=8 * MIB),
        cost_estimate=FREE,
        name="project_grads",
    )(rows, basis, block, *after)


def project_acts(flags, acts, basis, first, width, given, after):
    count, depth = acts.shape
    tokens = count // 4
    step = 512
    steps = width // step

    def body(flags_ref, acts_ref, basis_ref, *refs):
        given_refs, outs = refs[:len(given)], refs[len(given) + len(after):]
        keeps, gives = outs[:steps], outs[steps:]
        j = pl.program_id(0)

        @pl.when(j == 0)
        def _():
            for old, new in zip(given_refs, gives):
                new[...] = old[...]

        part = jnp.dot(acts_ref[...], basis_ref[...], preferred_element_type=F32).astype(BF16)
        for own in range(2):
            for i in range(steps):
                @pl.when((flags_ref[2] == own) & (j == i))
                def _(own=own, i=i):
                    for chip in range(2):
                        to = slice(chip * tokens, (chip + 1) * tokens)
                        mine, other = 2 * chip + own, 2 * chip + 1 - own
                        keeps[i][to, :] = part[mine * tokens:(mine + 1) * tokens]
                        gives[len(given) + i][to, :] = part[other * tokens:(other + 1) * tokens]

    n = 2 * steps + len(given)
    return pl.pallas_call(
        body,
        grid_spec=pltpu.PrefetchScalarGridSpec(
            num_scalar_prefetch=1,
            grid=(steps,),
            in_specs=[
                VMEM,
                pl.BlockSpec((depth, step), lambda j, c: (0, first // step + j)),
            ]
            + [VMEM] * len(given)
            + [ANYWHERE] * len(after),
            out_specs=[VMEM] * n,
        ),
        out_shape=[pltpu.VMEM((count // 2, step), BF16)] * n,
        compiler_params=pltpu.CompilerParams(vmem_limit_bytes=12 * MIB),
        cost_estimate=FREE,
        name="project_acts",
    )(
        flags,
        acts,
        pltpu.with_memory_space_constraint(basis, pltpu.HBM),
        *given,
        *after,
    )


def correct(flags, act_sq, pieces, first, total_width, result, after):
    height, tokens = act_sq.shape
    half, chunk = pieces[0][0].shape
    flat = [a for piece in pieces for a in piece]
    width = chunk * len(pieces)
    extra = list(after) if result is None else [result, *after]
    rows = height // (2 * len(pieces))

    def body(flags_ref, act_ref, *refs):
        ins = refs[:len(flat)]
        out, done, grad_sq, held, sems = refs[len(flat) + len(extra):]
        done[...] = jnp.zeros_like(done)
        for from_other in range(2):
            @pl.when(flags_ref[0] == from_other)
            def _(from_other=from_other):
                for i in range(len(pieces)):
                    at = slice(i * chunk, (i + 1) * chunk)
                    grad_sq[:half, at] = ins[4 * i + from_other][...]
                    grad_sq[half:, at] = ins[4 * i + 2 + from_other][...]

        def copy(r):
            at = pl.ds(pl.multiple_of(r * rows, rows), rows)
            slot = lax.rem(r, 2)
            return pltpu.make_async_copy(held.at[slot], out.at[at, pl.ds(first, width)], sems.at[slot])

        @pl.loop(0, height // rows)
        def _(r):
            act = act_ref[pl.ds(pl.multiple_of(r * rows, rows), rows), :]
            total = jnp.dot(act, grad_sq[...], preferred_element_type=F32)

            @pl.when(r >= 2)
            def _():
                copy(r - 2).wait()

            held[lax.rem(r, 2)] = (total * (1.0 / tokens)).astype(BF16)
            copy(r).start()

        copy(height // rows - 2).wait()
        copy(height // rows - 1).wait()

    return pl.pallas_call(
        body,
        in_specs=[pl.BlockSpec(memory_space=pltpu.SMEM)] + [VMEM] * (1 + len(flat)) + [ANYWHERE] * len(extra),
        out_specs=[ANYWHERE, VMEM],
        out_shape=[pltpu.HBM((height, total_width), BF16), pltpu.VMEM((16, 128), BF16)],
        scratch_shapes=[
            pltpu.VMEM((tokens, width), BF16),
            pltpu.VMEM((2, rows, width), BF16),
            pltpu.SemaphoreType.DMA((2,)),
        ],
        input_output_aliases={} if result is None else {2 + len(flat): 0},
        compiler_params=pltpu.CompilerParams(vmem_limit_bytes=12 * MIB),
        cost_estimate=FREE,
        name="correct",
    )(flags, act_sq, *flat, *extra)


CORES = [(0, 1), (1, 0), (2, 3), (3, 2)]
CHIPS = [(0, 2), (2, 0), (1, 3), (3, 1)]
OUTER = [(0, 1), (1, 0), (2, 3), (3, 2)]
INNER = [(1, 2), (2, 1), (5, 6), (6, 5), (0, 4), (4, 0), (3, 7), (7, 3)]


def lined(acts, grads, act_basis, grad_basis):
    chunk = 512
    lag = 3
    width = grad_basis.shape[1]
    half = width // chunk
    count = 2 * half
    place = lax.axis_index("gr")
    chip, core = lax.axis_index("gc") // 2, lax.axis_index("gc") % 2
    is_outer = (place == 0) | (place == 3)
    flags = jnp.stack([is_outer.astype(jnp.int32), chip.astype(jnp.int32), core.astype(jnp.int32)])

    near = lax.ppermute(grads, "gc", CORES)
    last = (flags,)
    block = None
    parts, payloads, received, sums, others = [], [], [], [], []

    def project_next(rows):
        nonlocal last, block
        k = len(parts)
        then = (k + 1) % half * chunk if k + 1 < count else None
        part, *blocks = project(rows, grad_basis, block, then, last)
        block = blocks[0] if blocks else None
        parts.append(part)
        last = (part,)

    def send(k):
        nonlocal last
        j = k - lag
        if k < lag:
            payload = parts[k]
        else:
            shape = sums[j].shape
            if k < count:
                (payload,) = whole(
                    square_or_term_body, [shape], flags, [sums[j], others[j], parts[k]], last, "square"
                )
            else:
                (payload,) = whole(square_body, [shape], flags, [sums[j], others[j]], last, "square")
            last = (payload,)
        payloads.append(payload)
        received.append(lax.ppermute(payload, "gr", OUTER))

    def add(k):
        nonlocal last
        sums.extend(whole(add_body, [parts[k].shape], flags, [parts[k], received[k]], last, "add"))
        last = (sums[-1],)
        others.append(lax.ppermute(sums[-1], ("layers", "gr"), INNER))

    result = None
    done = 0

    def correct_next(n):
        nonlocal last, result, done
        pieces = [
            (payloads[j + lag], received[j + lag], payloads[half + j + lag], received[half + j + lag])
            for j in range(done, done + n)
        ]
        result, token = correct(flags, act_sq, pieces, done * chunk, width, result, last)
        last = (token,)
        done += n

    def small(body, shapes, arrays, name):
        nonlocal last
        out = whole(body, shapes, flags, arrays, last, name)
        last = (out[-1],)
        return out

    far = lax.ppermute(grads, "gc", CHIPS)
    columns = act_basis.shape[1]
    block = fetch(grad_basis, chunk, last)
    last = (block,)
    rows = join([pltpu.with_memory_space_constraint(grads, pltpu.HBM)], [near], last)
    last = (rows,)
    project_next(rows)
    send(0)
    act_terms = list(project_acts(flags, acts, act_basis, 0, columns, [], last))
    keep, give = act_terms[:len(act_terms) // 2], act_terms[len(act_terms) // 2:]
    last = (keep[-1],)
    taken = [lax.ppermute(piece, "gc", CORES) for piece in give]
    project_next(rows)
    send(1)
    project_next(rows)
    send(2)
    add(0)
    (act,) = small(add_pieces_body, [(keep[0].shape[0], columns)], [*keep, *taken], "add")
    act_far = lax.ppermute(act, "gc", CHIPS)
    project_next(rows)
    for k in (1, 2, 3):
        add(k)
        project_next(rows)
        send(k + 2)
    far_pieces = split(far, [far.shape[1] // 7] * 7, last)
    last = (far_pieces[-1],)
    far_near = [lax.ppermute(piece, "gc", CORES) for piece in far_pieces]
    add(4)
    send(6)
    rows = join([far], far_near, last)
    last = (rows,)
    project_next(rows)
    add(5)
    send(7)
    for k in range(6, 12):
        add(k)
        project_next(rows)
        send(k + 2)
        if k == 9:
            own = small(square_pieces_body, [(act.shape[0], columns // 2)] * 2, [act, act_far], "square")
            other = [lax.ppermute(piece, "gc", CORES) for piece in own]
    add(12)
    send(14)
    (act_sq,) = small(stack_body, [(columns, 2 * act.shape[0])], [*own, *other], "stack")
    correct_next(1)
    add(13)
    send(15)
    correct_next(2)
    send(16)
    correct_next(2)
    correct_next(1)
    correct_next(1)
    return result


def solution(mesh):
    in_specs = (
        P("layers", "gc"),
        P(("layers", "gc"), "gr"),
        P(("layers", "gc"), "gr"),
        P(("layers", "gr"), "gc"),
    )
    out_specs = P(("layers", "gr"), "gc")
    sizes = (mesh.shape["layers"], mesh.shape["gr"], mesh.shape["gc"])
    shards = lined if sizes == (2, 4, 4) else gathered
    return jax.shard_map(shards, mesh=mesh, in_specs=in_specs, out_specs=out_specs, check_vma=False)
```

```python
import functools

import jax
import jax.numpy as jnp
from jax import lax
from jax.experimental import pallas as pl
from jax.experimental.pallas import tpu as pltpu
from jax.sharding import PartitionSpec as P

BF16 = jnp.bfloat16
F32 = jnp.float32
MIB = 2**20


def token_product(left, right):
    return lax.dot_general(
        left, right, (((0,), (0,)), ((), ())), preferred_element_type=F32
    )


def gathered(acts, grads, act_basis, grad_basis):
    token_count = acts.shape[0]
    grad_partial = jnp.dot(
        lax.all_gather(grads, "gc", axis=0, tiled=True),
        grad_basis,
        preferred_element_type=F32,
    )
    act_share = lax.psum_scatter(
        jnp.dot(acts, act_basis, preferred_element_type=F32),
        "gc",
        scatter_dimension=0,
        tiled=True,
    )
    act_sq = (act_share * act_share).astype(BF16)
    grad_share = lax.psum_scatter(grad_partial, "gr", scatter_dimension=0, tiled=True)
    grad_sq = (grad_share * grad_share).astype(BF16)
    grad_all = lax.all_gather(grad_sq, "gr", axis=0, tiled=True)
    total = token_product(lax.all_gather(act_sq, "gc", axis=0, tiled=True), grad_all)
    return (total / token_count).astype(BF16)


FREE = pl.CostEstimate(flops=10**7, bytes_accessed=10**5, transcendentals=0)
VMEM = pl.BlockSpec(memory_space=pltpu.VMEM)
ANYWHERE = pl.BlockSpec(memory_space=pl.ANY)


def ordered(array, *after):
    def body(*refs):
        pass

    return pl.pallas_call(
        body,
        in_specs=[ANYWHERE] * (1 + len(after)),
        out_specs=ANYWHERE,
        out_shape=jax.ShapeDtypeStruct(array.shape, array.dtype),
        input_output_aliases={0: 0},
        compiler_params=pltpu.CompilerParams(vmem_limit_bytes=MIB),
        cost_estimate=FREE,
        name="ordered",
    )(array, *after)


def whole(body, out_shape, flags, arrays, after, name, limit=8):
    def run(flags_ref, *refs):
        body(flags_ref, *refs[:len(arrays)], *refs[len(arrays) + len(after):])

    return pl.pallas_call(
        run,
        in_specs=[pl.BlockSpec(memory_space=pltpu.SMEM)] + [VMEM] * len(arrays) + [ANYWHERE] * len(after),
        out_specs=[VMEM] * len(out_shape),
        out_shape=[pltpu.VMEM(shape, BF16) for shape in out_shape],
        compiler_params=pltpu.CompilerParams(vmem_limit_bytes=limit * MIB),
        name=name,
    )(flags, *arrays, *after)


def add_body(flags, left, right, out):
    out[...] = (left[...].astype(F32) + right[...].astype(F32)).astype(BF16)


def square_body(flags, left, right, out):
    t = left[...].astype(F32) + right[...].astype(F32)
    out[...] = (t * t).astype(BF16)


def square_or_term_body(flags, left, right, term, out):
    @pl.when(flags[0] == 0)
    def _():
        square_body(flags, left, right, out)

    @pl.when(flags[0] == 1)
    def _():
        out[...] = term[...]


def add_pieces_body(flags, *refs):
    n = len(refs) // 2
    width = refs[0].shape[1]
    for i in range(n):
        add_body(flags, refs[i], refs[n + i], refs[2 * n].at[:, i * width:(i + 1) * width])


def square_pieces_body(flags, left, right, *outs):
    width = outs[0].shape[1]
    for i, out in enumerate(outs):
        at = slice(i * width, (i + 1) * width)
        square_body(flags, left.at[:, at], right.at[:, at], out)


def stack_body(flags, *refs):
    n = len(refs) // 2
    own, other, out = refs[:n], refs[n:2 * n], refs[2 * n]
    block, width = own[0].shape[0] // 2, own[0].shape[1]
    for chip in range(2):
        @pl.when(flags[1] == chip)
        def _(chip=chip):
            for i in range(n):
                rows = []
                for which in (chip, 1 - chip):
                    at = slice(which * block, (which + 1) * block)
                    rows += [own[i][at], other[i][at]]
                out[i * width:(i + 1) * width, :] = jnp.concatenate(rows).T


def split(array, widths, after):
    rows = array.shape[0]

    def body(array_ref, *refs):
        outs, sems = refs[len(after):-1], refs[-1]
        at, copies = 0, []
        for i, out in enumerate(outs):
            copies.append(pltpu.make_async_copy(array_ref.at[:, pl.ds(at, widths[i])], out, sems.at[i]))
            at += widths[i]
        start(copies)
        wait(copies)

    return pl.pallas_call(
        body,
        in_specs=[ANYWHERE] * (1 + len(after)),
        out_specs=[VMEM] * len(widths),
        out_shape=[pltpu.VMEM((rows, width), BF16) for width in widths],
        scratch_shapes=[pltpu.SemaphoreType.DMA((len(widths),))],
        compiler_params=pltpu.CompilerParams(vmem_limit_bytes=2 * MIB),
        cost_estimate=FREE,
        name="split",
    )(array, *after)


def join(top, bottom, after):
    count = top[0].shape[0]
    depth = sum(piece.shape[1] for piece in top)
    n = len(top) + len(bottom)

    def body(*refs):
        out, sems = refs[n + len(after):]
        copies = []
        for first, row, pieces in ((0, 0, top), (len(top), count, bottom)):
            at = 0
            for i, piece in enumerate(pieces):
                width = piece.shape[1]
                to = out.at[pl.ds(row, count), pl.ds(at, width)]
                copies.append(pltpu.make_async_copy(refs[first + i], to, sems.at[first + i]))
                at += width
        start(copies)
        wait(copies)

    return pl.pallas_call(
        body,
        in_specs=[ANYWHERE] * (n + len(after)),
        out_specs=VMEM,
        out_shape=pltpu.VMEM((2 * count, depth), BF16),
        scratch_shapes=[pltpu.SemaphoreType.DMA((n,))],
        compiler_params=pltpu.CompilerParams(vmem_limit_bytes=2 * MIB),
        cost_estimate=FREE,
        name="join",
    )(*top, *bottom, *after)


def block_copies(basis_ref, first, out, sems):
    parts = sems.shape[0]
    rows = out.shape[0] // parts
    return [
        pltpu.make_async_copy(
            basis_ref.at[pl.ds(i * rows, rows), pl.ds(first, out.shape[1])], out.at[pl.ds(i * rows, rows)], sems.at[i]
        )
        for i in range(parts)
    ]


def start(copies):
    for copy in copies:
        copy.start()


def wait(copies):
    for copy in copies:
        copy.wait()


COPIES = 7


def fetch(basis, width, after):
    depth = basis.shape[0]

    def body(basis_ref, *refs):
        out, sems = refs[len(after):]
        copies = block_copies(basis_ref, 0, out, sems)
        start(copies)
        wait(copies)

    return pl.pallas_call(
        body,
        in_specs=[ANYWHERE] * (1 + len(after)),
        out_specs=VMEM,
        out_shape=pltpu.VMEM((depth, width), BF16),
        scratch_shapes=[pltpu.SemaphoreType.DMA((COPIES,))],
        compiler_params=pltpu.CompilerParams(vmem_limit_bytes=2 * MIB),
        cost_estimate=FREE,
        name="fetch",
    )(basis, *after)


def project(rows, basis, block, then, after):
    count, depth = rows.shape
    width = block.shape[1]
    fetches = then is not None
    step = depth // 2

    def body(rows_ref, basis_ref, block_ref, *refs):
        refs = refs[len(after):]
        if fetches:
            ahead = block_copies(basis_ref, then, refs[1], refs[2])
            start(ahead)

        def add(i, total):
            at = pl.ds(pl.multiple_of(i * step, step), step)
            return total + jnp.dot(rows_ref[:, at], block_ref[at, :], preferred_element_type=F32)

        refs[0][...] = lax.fori_loop(0, depth // step, add, jnp.zeros((count, width), F32)).astype(BF16)
        if fetches:
            wait(ahead)

    shapes = [pltpu.VMEM((count, width), BF16)] + [pltpu.VMEM((depth, width), BF16)] * fetches
    return pl.pallas_call(
        body,
        in_specs=[VMEM, ANYWHERE, VMEM] + [ANYWHERE] * len(after),
        out_specs=[VMEM] * len(shapes),
        out_shape=shapes,
        scratch_shapes=[pltpu.SemaphoreType.DMA((COPIES,))] * fetches,
        compiler_params=pltpu.CompilerParams(vmem_limit_bytes=8 * MIB),
        cost_estimate=FREE,
        name="project_grads",
    )(rows, basis, block, *after)


def project_acts(flags, acts, basis, first, width, given, after):
    count, depth = acts.shape
    tokens = count // 4
    step = 512
    steps = width // step

    def body(flags_ref, acts_ref, basis_ref, *refs):
        given_refs, outs = refs[:len(given)], refs[len(given) + len(after):]
        keeps, gives = outs[:steps], outs[steps:]
        j = pl.program_id(0)

        @pl.when(j == 0)
        def _():
            for old, new in zip(given_refs, gives):
                new[...] = old[...]

        part = jnp.dot(acts_ref[...], basis_ref[...], preferred_element_type=F32).astype(BF16)
        for own in range(2):
            for i in range(steps):
                @pl.when((flags_ref[2] == own) & (j == i))
                def _(own=own, i=i):
                    for chip in range(2):
                        to = slice(chip * tokens, (chip + 1) * tokens)
                        mine, other = 2 * chip + own, 2 * chip + 1 - own
                        keeps[i][to, :] = part[mine * tokens:(mine + 1) * tokens]
                        gives[len(given) + i][to, :] = part[other * tokens:(other + 1) * tokens]

    n = 2 * steps + len(given)
    return pl.pallas_call(
        body,
        grid_spec=pltpu.PrefetchScalarGridSpec(
            num_scalar_prefetch=1,
            grid=(steps,),
            in_specs=[
                VMEM,
                pl.BlockSpec((depth, step), lambda j, c: (0, first // step + j)),
            ]
            + [VMEM] * len(given)
            + [ANYWHERE] * len(after),
            out_specs=[VMEM] * n,
        ),
        out_shape=[pltpu.VMEM((count // 2, step), BF16)] * n,
        compiler_params=pltpu.CompilerParams(vmem_limit_bytes=12 * MIB),
        cost_estimate=FREE,
        name="project_acts",
    )(
        flags,
        acts,
        pltpu.with_memory_space_constraint(basis, pltpu.HBM),
        *given,
        *after,
    )


def correct(flags, act_sq, pieces, first, total_width, result, after):
    height, tokens = act_sq.shape
    half, chunk = pieces[0][0].shape
    flat = [a for piece in pieces for a in piece]
    width = chunk * len(pieces)
    extra = list(after) if result is None else [result, *after]
    rows = height // (2 * len(pieces))

    def body(flags_ref, act_ref, *refs):
        ins = refs[:len(flat)]
        out, done, grad_sq, held, sems = refs[len(flat) + len(extra):]
        done[...] = jnp.zeros_like(done)
        for from_other in range(2):
            @pl.when(flags_ref[0] == from_other)
            def _(from_other=from_other):
                for i in range(len(pieces)):
                    at = slice(i * chunk, (i + 1) * chunk)
                    grad_sq[:half, at] = ins[4 * i + from_other][...]
                    grad_sq[half:, at] = ins[4 * i + 2 + from_other][...]

        def copy(r):
            at = pl.ds(pl.multiple_of(r * rows, rows), rows)
            slot = lax.rem(r, 2)
            return pltpu.make_async_copy(held.at[slot], out.at[at, pl.ds(first, width)], sems.at[slot])

        @pl.loop(0, height // rows)
        def _(r):
            act = act_ref[pl.ds(pl.multiple_of(r * rows, rows), rows), :]
            total = jnp.dot(act, grad_sq[...], preferred_element_type=F32)

            @pl.when(r >= 2)
            def _():
                copy(r - 2).wait()

            held[lax.rem(r, 2)] = (total * (1.0 / tokens)).astype(BF16)
            copy(r).start()

        copy(height // rows - 2).wait()
        copy(height // rows - 1).wait()

    return pl.pallas_call(
        body,
        in_specs=[pl.BlockSpec(memory_space=pltpu.SMEM)] + [VMEM] * (1 + len(flat)) + [ANYWHERE] * len(extra),
        out_specs=[ANYWHERE, VMEM],
        out_shape=[pltpu.HBM((height, total_width), BF16), pltpu.VMEM((16, 128), BF16)],
        scratch_shapes=[
            pltpu.VMEM((tokens, width), BF16),
            pltpu.VMEM((2, rows, width), BF16),
            pltpu.SemaphoreType.DMA((2,)),
        ],
        input_output_aliases={} if result is None else {2 + len(flat): 0},
        compiler_params=pltpu.CompilerParams(vmem_limit_bytes=12 * MIB),
        cost_estimate=FREE,
        name="correct",
    )(flags, act_sq, *flat, *extra)


CORES = [(0, 1), (1, 0), (2, 3), (3, 2)]
CHIPS = [(0, 2), (2, 0), (1, 3), (3, 1)]
OUTER = [(0, 1), (1, 0), (2, 3), (3, 2)]
INNER = [(1, 2), (2, 1), (5, 6), (6, 5), (0, 4), (4, 0), (3, 7), (7, 3)]


def lined(acts, grads, act_basis, grad_basis):
    chunk = 512
    lag = 3
    width = grad_basis.shape[1]
    half = width // chunk
    count = 2 * half
    place = lax.axis_index("gr")
    chip, core = lax.axis_index("gc") // 2, lax.axis_index("gc") % 2
    is_outer = (place == 0) | (place == 3)
    flags = jnp.stack([is_outer.astype(jnp.int32), chip.astype(jnp.int32), core.astype(jnp.int32)])

    near = lax.ppermute(grads, "gc", CORES)
    last = (flags,)
    block = None
    parts, payloads, received, sums, others = [], [], [], [], []

    def project_next(rows):
        nonlocal last, block
        k = len(parts)
        then = (k + 1) % half * chunk if k + 1 < count else None
        part, *blocks = project(rows, grad_basis, block, then, last)
        block = blocks[0] if blocks else None
        parts.append(part)
        last = (part,)

    def send(k):
        nonlocal last
        j = k - lag
        if k < lag:
            payload = parts[k]
        else:
            shape = sums[j].shape
            if k < count:
                (payload,) = whole(
                    square_or_term_body, [shape], flags, [sums[j], others[j], parts[k]], last, "square"
                )
            else:
                (payload,) = whole(square_body, [shape], flags, [sums[j], others[j]], last, "square")
            last = (payload,)
        payloads.append(payload)
        received.append(lax.ppermute(payload, "gr", OUTER))

    def add(k):
        nonlocal last
        sums.extend(whole(add_body, [parts[k].shape], flags, [parts[k], received[k]], last, "add"))
        last = (sums[-1],)
        others.append(lax.ppermute(sums[-1], ("layers", "gr"), INNER))

    result = None
    done = 0

    def correct_next(n):
        nonlocal last, result, done
        pieces = [
            (payloads[j + lag], received[j + lag], payloads[half + j + lag], received[half + j + lag])
            for j in range(done, done + n)
        ]
        result, token = correct(flags, act_sq, pieces, done * chunk, width, result, last)
        last = (token,)
        done += n

    def small(body, shapes, arrays, name):
        nonlocal last
        out = whole(body, shapes, flags, arrays, last, name)
        last = (out[-1],)
        return out

    far = lax.ppermute(grads, "gc", CHIPS)
    columns = act_basis.shape[1]
    block = fetch(grad_basis, chunk, last)
    last = (block,)
    rows = join([pltpu.with_memory_space_constraint(grads, pltpu.HBM)], [near], last)
    last = (rows,)
    project_next(rows)
    send(0)
    act_terms = list(project_acts(flags, acts, act_basis, 0, columns, [], last))
    keep, give = act_terms[:len(act_terms) // 2], act_terms[len(act_terms) // 2:]
    last = (keep[-1],)
    taken = [lax.ppermute(piece, "gc", CORES) for piece in give]
    project_next(rows)
    send(1)
    project_next(rows)
    send(2)
    add(0)
    (act,) = small(add_pieces_body, [(keep[0].shape[0], columns)], [*keep, *taken], "add")
    act_far = lax.ppermute(act, "gc", CHIPS)
    project_next(rows)
    for k in (1, 2, 3):
        add(k)
        project_next(rows)
        send(k + 2)
    far_pieces = split(far, [far.shape[1] // 7] * 7, last)
    last = (far_pieces[-1],)
    far_near = [lax.ppermute(piece, "gc", CORES) for piece in far_pieces]
    add(4)
    send(6)
    rows = join([far], far_near, last)
    last = (rows,)
    project_next(rows)
    add(5)
    send(7)
    for k in range(6, 12):
        add(k)
        project_next(rows)
        send(k + 2)
        if k == 9:
            own = small(square_pieces_body, [(act.shape[0], columns // 2)] * 2, [act, act_far], "square")
            other = [lax.ppermute(piece, "gc", CORES) for piece in own]
    (act_sq,) = small(stack_body, [(columns, 2 * act.shape[0])], [*own, *other], "stack")
    add(12)
    send(14)
    correct_next(1)
    add(13)
    send(15)
    correct_next(2)
    send(16)
    correct_next(2)
    correct_next(1)
    correct_next(1)
    return result


def solution(mesh):
    in_specs = (
        P("layers", "gc"),
        P(("layers", "gc"), "gr"),
        P(("layers", "gc"), "gr"),
        P(("layers", "gr"), "gc"),
    )
    out_specs = P(("layers", "gr"), "gc")
    sizes = (mesh.shape["layers"], mesh.shape["gr"], mesh.shape["gc"])
    shards = lined if sizes == (2, 4, 4) else gathered
    return jax.shard_map(shards, mesh=mesh, in_specs=in_specs, out_specs=out_specs, check_vma=False)
```
